128 devices in a mesh: rows: 32 (over x, y, z_hi), cols: 4 (over z_lo, core).
Axes of the slice: x: 4, y: 4, z: 4 (z_hi: 2, z_lo: 2; z = z_hi * 2 + z_lo), core: 2. Of those that a mesh axis runs over, the one named last changes fastest.
Arguments:
- queries: bfloat16 [256, 1536, 128], P('rows', 'cols'), may hold values from -3 to 3
- keys: bfloat16 [256, 1536, 128], P('rows', 'cols'), may hold values from -3 to 3
- values: bfloat16 [256, 1536, 128], P('rows', 'cols'), may hold values from -4 to 4
- out_grad: bfloat16 [256, 1536, 128], P('rows', 'cols'), may hold values from -16 to 16
- pair_bias: bfloat16 [1536, 4, 1536], P(None, None, 'cols'), may hold values from -4 to 4
- token_mask: int32 [1536], replicated, may hold values from 0 to 1, as said below
- span_index: int32 [32], P('rows'), may hold values from 0 to 191
Outputs:
- query_grad: bfloat16 [256, 1536, 128], P('rows', 'cols')
- key_grad: bfloat16 [256, 1536, 128], P('rows', 'cols')
- value_grad: bfloat16 [256, 1536, 128], P('rows', 'cols')
- bias_grad: float32 [1536, 4, 1536], P('rows', None, 'cols')
The draws below stay inside these ranges and needn't reach their ends.
Inputs may be any that keep to these rules, and one draw needn't show every extreme that they name: `token_mask`: every aligned block of 8 tokens holds a 1.
All inputs are finite; a program needn't handle non-finite values.
Results may differ from the reference program's by a relative error of at most 0.005.
Values may be sent and summed in bfloat16 or wider, within the bound.
No kernel may reach another device: no remote copies, remote signals or barrier semaphores. Data moves between devices by JAX's collectives and lax.ppermute only.
A program may use at most 192 MiB of HBM per device.

```python
import jax
import jax.numpy as jnp
from jax import lax

HEADS = 4
HEAD_DIM = 32
ROWS_DEV = 8
LEN = 1536
CH = 128
PAIR_ROWS = 256
N_ROWS = 32


def draw_token_mask(key, part):
    key = jax.random.fold_in(key, 11)
    levels = jax.random.randint(key, (LEN,), 0, 4)
    places = jnp.arange(LEN, dtype=jnp.int32)
    present = jnp.where(levels > 0, 1, 0)
    return jnp.where(places % 8 == 0, 1, present).astype(jnp.int32)


def place_ends(result, own_key, low, high):
    longest = result.shape.index(max(result.shape))
    spots = []
    for shift in (0, 1):
        where = [jax.random.randint(jax.random.fold_in(own_key, axis), (), 0, length) for axis, length in enumerate(result.shape)]
        where[longest] = (where[longest] + shift) % result.shape[longest]
        spots.append(tuple(where))
    return result.at[spots[0]].set(low).at[spots[1]].set(high)


def shard_levels(rng, dims, pieces, least, top_value):
    factor_of, own = 1.0, jax.random.fold_in(rng, 6)
    for axis_at, parts in pieces:
        steps = jnp.exp(jax.random.uniform(jax.random.fold_in(own, axis_at), (parts,), jnp.float32, least / len(pieces), top_value / len(pieces)))
        factor_of = factor_of * jnp.repeat(steps, dims[axis_at] // parts).reshape([-1 if axis == axis_at else 1 for axis in range(len(dims))])
    return factor_of


def scatter_about(own_key, shape, deviation, reach, pieces=(), kind=jnp.bfloat16):
    values = deviation * jax.random.normal(own_key, shape, jnp.float32)
    if pieces:
        values = values * shard_levels(own_key, shape, pieces, -0.22, 0.18)
    return jnp.clip(values, -reach, reach).astype(kind)


def setup_inputs(seed: int = 0) -> dict:
    splits = jax.random.split(jax.random.key(seed), 8)
    queries = scatter_about(splits[0], (PAIR_ROWS, LEN, CH), 0.5, 3.0, ((0, 32), (1, 4)))
    keys = scatter_about(splits[1], (PAIR_ROWS, LEN, CH), 0.5, 3.0, ((0, 32), (1, 4)))
    values = scatter_about(splits[2], (PAIR_ROWS, LEN, CH), 1.0, 4.0, ((0, 32), (1, 4)))
    out_grad = scatter_about(splits[3], (PAIR_ROWS, LEN, CH), 4.0, 16.0, ((0, 32), (1, 4)))
    pair_bias = scatter_about(splits[4], (LEN, HEADS, LEN), 1.0, 4.0, ((2, 4),))
    token_mask = draw_token_mask(jax.random.fold_in(splits[7], 71), 0)
    span_index = place_ends(jax.random.randint(splits[6], (N_ROWS,), 0, LEN // 8), jax.random.fold_in(splits[6], 1), 0, (LEN // 8) - 1).astype(jnp.int32)
    return dict(queries=queries, keys=keys, values=values, out_grad=out_grad, pair_bias=pair_bias, token_mask=token_mask, span_index=span_index)


def reference(queries, keys, values, out_grad, pair_bias, token_mask, span_index):
    score_scale = HEAD_DIM ** -0.5
    token_rows = (span_index[:, None] * ROWS_DEV + jnp.arange(ROWS_DEV, dtype=jnp.int32)[None, :]).reshape(-1)
    row_keep = token_mask[token_rows]
    key_keep = token_mask > 0
    bias_full = pair_bias.astype(jnp.float32)

    def one_row(bias_sum, row_data):
        query, key, value, grad, keep_flag = row_data
        query_heads = query.astype(jnp.float32).reshape(LEN, HEADS, HEAD_DIM)
        key_heads = key.astype(jnp.float32).reshape(LEN, HEADS, HEAD_DIM)
        value_heads = value.astype(jnp.float32).reshape(LEN, HEADS, HEAD_DIM)
        masked = grad * keep_flag.astype(jnp.bfloat16)
        grad_heads = masked.astype(jnp.float32).reshape(LEN, HEADS, HEAD_DIM)
        scores = jnp.einsum("jhd,khd->jhk", query_heads, key_heads) * score_scale + bias_full
        exponent = jnp.where(key_keep[None, None, :], jnp.exp(scores), jnp.float32(0.0))
        slopes = jnp.einsum("jhd,khd->jhk", grad_heads, value_heads)
        totals = jnp.sum(exponent, axis=-1)
        weighted = jnp.sum(exponent * slopes, axis=-1)
        chances = exponent / totals[..., None]
        row_delta = weighted / totals
        score_grad = chances * (slopes - row_delta[..., None])
        chances_low = lax.optimization_barrier(chances.astype(jnp.bfloat16)).astype(jnp.float32)
        grad_low = lax.optimization_barrier(score_grad.astype(jnp.bfloat16)).astype(jnp.float32)
        value_term = jnp.einsum("jhk,jhd->khd", chances_low, grad_heads)
        key_term = jnp.einsum("jhk,jhd->khd", grad_low, query_heads) * score_scale
        query_term = jnp.einsum("jhk,khd->jhd", grad_low, key_heads) * score_scale
        outputs = (query_term.reshape(LEN, CH).astype(jnp.bfloat16),
                   key_term.reshape(LEN, CH).astype(jnp.bfloat16),
                   value_term.reshape(LEN, CH).astype(jnp.bfloat16))
        return bias_sum + score_grad, outputs

    start_sum = jnp.zeros((LEN, HEADS, LEN), jnp.float32)
    bias_grad, grads = lax.scan(one_row, start_sum, (queries, keys, values, out_grad, row_keep))
    return grads[0], grads[1], grads[2], bias_grad
```

```python
import functools

import jax
import jax.numpy as jnp
from jax import lax
from jax.experimental import pallas as pl
from jax.experimental.pallas import tpu as pltpu
from jax.sharding import PartitionSpec as P

HEADS = 4
HEAD_DIM = 32
CH = HEADS * HEAD_DIM
SCALE = HEAD_DIM**-0.5
LOG2E = 1.4426950408889634
CHUNKS = 3
TILE = 256
VMEM = 60 * 2**20
NT = (((1,), (1,)), ((), ()))
F32 = jnp.float32
BF16 = jnp.bfloat16


def only_head(x, h):
    lane = lax.broadcasted_iota(jnp.int32, x.shape, 1)
    return jnp.where((lane // HEAD_DIM) == h, x, jnp.zeros_like(x))


def joined(parts, which):
    return jnp.concatenate([part[which, 0] for part in parts], axis=0)


def totals_kernel(*refs):
    parts, (k_ref, v_ref, bias_ref, out_ref, e_ref) = refs[:4], refs[4:]
    q, g = joined(parts, 0), joined(parts, 1)
    k = k_ref[0]
    for h in range(HEADS):
        s = lax.dot_general(k, only_head(q, h), NT, preferred_element_type=F32)
        e_ref[h] = jnp.exp2(s * (SCALE * LOG2E) + bias_ref[h]).astype(BF16)
    gt = g.T.astype(F32)
    vt = v_ref[0].T
    ones = jnp.ones((16, vt.shape[1]), BF16)
    for h in range(HEADS):
        rows = slice(h * HEAD_DIM, (h + 1) * HEAD_DIM)
        o = jnp.dot(jnp.concatenate([vt[rows], ones], axis=0), e_ref[h], preferred_element_type=F32)
        out_ref[0, h : h + 1] = o[HEAD_DIM : HEAD_DIM + 1]
        out_ref[0, HEADS + h : HEADS + h + 1] = jnp.sum(o[:HEAD_DIM] * gt[rows], axis=0, keepdims=True)


def part_specs(row_len):
    return [pl.BlockSpec((2, 1, row_len, CH), lambda i: (0, i, 0, 0))] * 4


def totals(parts, keys, values, bias_t):
    rows, key_len, _ = keys.shape
    part_len = parts[0].shape[2]
    count = 4 * part_len
    per_row = lambda i: (i, 0, 0)
    work = rows * count * HEADS * key_len
    return pl.pallas_call(
        totals_kernel,
        grid=(rows,),
        in_specs=part_specs(part_len)
        + [
            pl.BlockSpec((1, key_len, CH), per_row),
            pl.BlockSpec((1, key_len, CH), per_row),
            pl.BlockSpec((HEADS, key_len, count), lambda i: (0, 0, 0)),
        ],
        out_specs=pl.BlockSpec((1, 2 * HEADS, count), per_row),
        out_shape=jax.ShapeDtypeStruct((rows, 2 * HEADS, count), F32),
        scratch_shapes=[pltpu.VMEM((HEADS, key_len, count), BF16)],
        compiler_params=pltpu.CompilerParams(vmem_limit_bytes=VMEM),
        cost_estimate=pl.CostEstimate(flops=work * 512 * 3, bytes_accessed=2**20, transcendentals=work),
        name="totals",
    )(*parts, keys, values, bias_t)


def split(x):
    a = x.astype(BF16)
    rest = x - a.astype(F32)
    b = rest.astype(BF16)
    return [y.astype(F32) for y in (a, b, (rest - b.astype(F32)).astype(BF16))]


def grads_kernel(first, last, *refs):
    parts, refs = refs[:4], refs[4:]
    k_ref, v_ref, bias_ref, stat_ref, *refs = refs
    if not first:
        dk_in, dv_in, *refs = refs
    dq_ref, dk_out, dv_out, db_ref, kx_ref, vx_ref, sum_ref, p_ref, ds_ref, dk_ref, dv_ref = refs
    i = pl.program_id(0)
    q, g = joined(parts, 0), joined(parts, 1)
    count, key_len = q.shape[0], k_ref.shape[1]
    width = HEADS * key_len

    @pl.when(i == 0)
    def start():
        sum_ref[...] = jnp.zeros(sum_ref.shape, F32)
        lane = lax.broadcasted_iota(jnp.int32, (key_len, CH), 1)
        for h in range(HEADS):
            rows = slice(h * key_len, (h + 1) * key_len)
            for ref, at in ((kx_ref, h), (vx_ref, HEADS + h)):
                hit = (lane < 6 * HEADS) & (lane % (2 * HEADS) == at)
                ref[rows, CH:] = jnp.where(hit, -1.0, 0.0).astype(BF16)

    k, v = k_ref[0], v_ref[0]
    for h in range(HEADS):
        rows = slice(h * key_len, (h + 1) * key_len)
        kx_ref[rows, :CH] = only_head(k, h)
        vx_ref[rows, :CH] = only_head(v, h)

    stat = stat_ref[0]
    total = stat[:HEADS]
    level = jnp.log(total) * (1.0 / SCALE)
    delta = stat[HEADS:] / total
    pieces = split(jnp.concatenate([level, delta], axis=0))
    extra = jnp.concatenate(pieces + [jnp.zeros((CH - 6 * HEADS, count), F32)], axis=0).T.astype(BF16)
    qx = jnp.concatenate([q, extra], axis=1)
    gx = jnp.concatenate([g, extra], axis=1)
    qt, gt = q.T, g.T
    dq = jnp.zeros((count, CH), F32)
    for n in range(width // TILE):
        at = slice(n * TILE, (n + 1) * TILE)
        s = lax.dot_general(qx, kx_ref[at], NT, preferred_element_type=F32)
        t = lax.dot_general(gx, vx_ref[at], NT, preferred_element_type=F32)
        p = jnp.exp2(s * (SCALE * LOG2E) + bias_ref[:, at])
        ds = p * t
        sum_ref[:, at] += ds
        low = ds.astype(BF16)
        p_ref[:, at] = p.astype(BF16)
        ds_ref[:, at] = low
        dq = dq + jnp.dot(low, kx_ref[at, :CH], preferred_element_type=F32)
    dq = (dq * SCALE).astype(BF16)
    part_len = count // 4
    for u in range(4):
        dq_ref[u, 0] = dq[u * part_len : (u + 1) * part_len]
    for h in range(HEADS):
        rows, at = slice(h * HEAD_DIM, (h + 1) * HEAD_DIM), slice(h * key_len, (h + 1) * key_len)
        dv = jnp.dot(gt[rows], p_ref[:, at], preferred_element_type=F32)
        dk = jnp.dot(qt[rows], ds_ref[:, at], preferred_element_type=F32)
        if not first:
            dv, dk = dv + dv_in[0, rows], dk + dk_in[0, rows]
        if last:
            dv_ref[rows] = dv
            dk_ref[rows] = dk * SCALE
        else:
            dv_out[0, rows] = dv
            dk_out[0, rows] = dk
    if last:
        dv_out[0] = dv_ref[...].T.astype(BF16)
        dk_out[0] = dk_ref[...].T.astype(BF16)

    @pl.when(i == pl.num_programs(0) - 1)
    def finish():
        db_ref[...] = sum_ref[...].astype(BF16)


def grads(parts, keys, values, bias, stats, carried, last):
    rows, key_len, _ = keys.shape
    part_len = parts[0].shape[2]
    count, width = 4 * part_len, HEADS * key_len
    per_row = lambda i: (i, 0, 0)
    whole = lambda i: (0, 0)
    side = pl.BlockSpec((1, CH, key_len), per_row)
    side_shape = jax.ShapeDtypeStruct((rows, CH, key_len), F32)
    final = pl.BlockSpec((1, key_len, CH), per_row)
    final_shape = jax.ShapeDtypeStruct((rows, key_len, CH), BF16)
    work = rows * count * width
    return pl.pallas_call(
        functools.partial(grads_kernel, not carried, last),
        grid=(rows,),
        in_specs=part_specs(part_len)
        + [
            pl.BlockSpec((1, key_len, CH), per_row),
            pl.BlockSpec((1, key_len, CH), per_row),
            pl.BlockSpec((count, width), whole),
            pl.BlockSpec((1, 2 * HEADS, count), per_row),
        ]
        + [side] * len(carried),
        out_specs=[
            pl.BlockSpec((4, 1, part_len, CH), lambda i: (0, i, 0, 0)),
            final if last else side,
            final if last else side,
            pl.BlockSpec((count, width), whole),
        ],
        out_shape=[
            jax.ShapeDtypeStruct((4, rows, part_len, CH), BF16),
            final_shape if last else side_shape,
            final_shape if last else side_shape,
            jax.ShapeDtypeStruct((count, width), BF16),
        ],
        scratch_shapes=[
            pltpu.VMEM((width, 2 * CH), BF16),
            pltpu.VMEM((width, 2 * CH), BF16),
            pltpu.VMEM((count, width), F32),
            pltpu.VMEM((count, width), BF16),
            pltpu.VMEM((count, width), BF16),
            pltpu.VMEM((CH, key_len), F32),
            pltpu.VMEM((CH, key_len), F32),
        ],
        compiler_params=pltpu.CompilerParams(vmem_limit_bytes=VMEM),
        cost_estimate=pl.CostEstimate(flops=work * 512 * 6, bytes_accessed=2**20, transcendentals=work),
        name="grads",
    )(*parts, keys, values, bias, stats, *carried)


def row_move(dx, dy, dz):
    pairs = []
    for r in range(32):
        x, y, z = r // 8, (r // 2) % 4, r % 2
        pairs.append((r, ((x + dx) % 4) * 8 + ((y + dy) % 4) * 2 + (z + dz) % 2))
    return pairs


def partner(x, distance):
    return lax.ppermute(x, "cols", [(c, c ^ distance) for c in range(4)])


def ring_sum(x, axis, here, own_of, move):
    kept = lax.dynamic_index_in_dim(x, own_of(here), axis, keepdims=False).astype(F32)
    for step in (1, 3, 2):
        there = (here + step) % 4
        sent = lax.dynamic_index_in_dim(x, own_of(there), axis, keepdims=False)
        kept = kept + lax.ppermute(sent, "rows", move(step)).astype(F32)
    return kept.astype(BF16)


def per_device(queries, keys, values, out_grad, pair_bias, token_mask, span_index):
    rows, key_len, _ = keys.shape
    col = lax.axis_index("cols")
    row = lax.axis_index("rows")
    x, y, z = row // 8, (row // 2) % 4, row % 2
    owners = 8
    span = key_len // owners
    step = span // CHUNKS
    part_len = owners * step
    count = 4 * part_len
    width = HEADS * key_len

    row_keep = lax.dynamic_slice_in_dim(token_mask, span_index[0] * rows, rows)
    masked = out_grad * row_keep.astype(BF16)[:, None, None]
    pairs = jnp.stack([queries, masked]).reshape(2, rows, owners, CHUNKS, step, CH)

    chunks = []
    for b in range(CHUNKS):
        own = pairs[:, :, :, b].reshape(2, rows, part_len, CH)
        across = partner(own, 2)
        chunks.append([own, partner(own, 1), across, partner(across, 1)])

    key_keep = lax.dynamic_slice_in_dim(token_mask, col * key_len, key_len) > 0
    blocks = pair_bias.reshape(4, owners, CHUNKS, step, HEADS, key_len)
    biases = []
    for b in range(CHUNKS):
        mine = [lax.dynamic_index_in_dim(blocks[:, :, b], col ^ u, 0, keepdims=False) for u in range(4)]
        mine = jnp.stack(mine).astype(F32) * LOG2E
        mine = jnp.where(key_keep, mine, F32(-1e30))
        mine = mine.reshape(count, width)
        biases.append((mine, mine.T.reshape(HEADS, key_len, count)))

    def summed_stats(stat):
        for distance in (1, 2):
            got = partner(stat, distance).reshape(rows, 2 * HEADS, 4, part_len)
            got = jnp.stack([got[:, :, u ^ distance] for u in range(4)], axis=2)
            stat = stat + got.reshape(stat.shape)
        return stat

    stats = [summed_stats(totals(chunks[b], keys, values, biases[b][1])) for b in range(CHUNKS)]

    carried = ()
    query_parts, bias_parts = [], []
    for b in range(CHUNKS):
        dq, dk, dv, db = grads(chunks[b], keys, values, biases[b][0], stats[b], carried, b == CHUNKS - 1)
        carried = (dk, dv)
        pair = dq[0::2].astype(F32) + partner(dq[1::2], 1).astype(F32)
        query_parts.append((pair[0] + partner(pair[1].astype(BF16), 2).astype(F32)).astype(BF16))
        db = db.reshape(4, 4, 2, step, width)
        half = step // 2
        ends = []
        for by_x in (True, False):
            piece = db[:, :, :, :half] if by_x else db[:, :, :, half:]
            along_x = lambda a: ring_sum(a, 0, x, lambda there: col ^ there, lambda d: row_move(d, 0, 0))
            along_y = lambda a, axis: ring_sum(a, axis, y, lambda there: there, lambda d: row_move(0, d, 0))
            piece = along_y(along_x(piece), 0) if by_x else along_x(along_y(piece, 1))
            kept = lax.dynamic_index_in_dim(piece, z, 0, keepdims=False).astype(F32)
            sent = lax.dynamic_index_in_dim(piece, 1 - z, 0, keepdims=False)
            ends.append(kept + lax.ppermute(sent, "rows", row_move(0, 0, 1)).astype(F32))
        bias_parts.append(jnp.concatenate(ends, axis=0))
    key_grad, value_grad = carried
    query_grad = jnp.stack(query_parts).reshape(CHUNKS, rows, owners, step, CH)
    query_grad = query_grad.transpose(1, 2, 0, 3, 4).reshape(rows, key_len, CH)
    bias_grad = jnp.concatenate(bias_parts, axis=0).reshape(span, HEADS, key_len)
    return (query_grad, key_grad, value_grad, bias_grad)


def solution(mesh):
    return jax.shard_map(
        per_device,
        mesh=mesh,
        in_specs=(
            P("rows", "cols", None),
            P("rows", "cols", None),
            P("rows", "cols", None),
            P("rows", "cols", None),
            P(None, None, "cols"),
            P(),
            P("rows"),
        ),
        out_specs=(
            P("rows", "cols", None),
            P("rows", "cols", None),
            P("rows", "cols", None),
            P("rows", None, "cols"),
        ),
        check_vma=False,
    )
```

```python
import functools

import jax
import jax.numpy as jnp
from jax import lax
from jax.experimental import pallas as pl
from jax.experimental.pallas import tpu as pltpu
from jax.sharding import PartitionSpec as P

HEADS = 4
HEAD_DIM = 32
CH = HEADS * HEAD_DIM
SCALE = HEAD_DIM**-0.5
LOG2E = 1.4426950408889634
CHUNKS = 3
TILE = 256
VMEM = 60 * 2**20
NT = (((1,), (1,)), ((), ()))
F32 = jnp.float32
BF16 = jnp.bfloat16


def only_head(x, h):
    lane = lax.broadcasted_iota(jnp.int32, x.shape, 1)
    return jnp.where((lane // HEAD_DIM) == h, x, jnp.zeros_like(x))


def joined(parts, which):
    return jnp.concatenate([part[which, 0] for part in parts], axis=0)


def bias_block(parts):
    parts = [part[0, :, 0].reshape(-1, part.shape[-1]) for part in parts]
    return jnp.concatenate(parts, axis=0).astype(F32) * LOG2E


def totals_kernel(col_ref, *refs):
    n = (len(refs) - 6) // 2
    parts, biases, (k_ref, v_ref, gate_ref, out_ref, e_ref, bias_ref) = refs[:n], refs[n : 2 * n], refs[2 * n :]
    q, g = joined(parts, 0), joined(parts, 1)
    k = k_ref[0]
    key_len = k.shape[0]

    @pl.when(pl.program_id(0) == 0)
    def start():
        bias = bias_block(biases)
        gate = jnp.concatenate([gate_ref[...]] * (q.shape[0] // CH), axis=1)
        for h in range(HEADS):
            bias_ref[h] = bias[:, h * key_len : (h + 1) * key_len].T + gate

    for h in range(HEADS):
        s = lax.dot_general(k, only_head(q, h), NT, preferred_element_type=F32)
        e_ref[h] = jnp.exp2(s * (SCALE * LOG2E) + bias_ref[h]).astype(BF16)
    gt = g.T.astype(F32)
    vt = v_ref[0].T
    ones = jnp.ones((16, key_len), BF16)
    for h in range(HEADS):
        rows = slice(h * HEAD_DIM, (h + 1) * HEAD_DIM)
        o = jnp.dot(jnp.concatenate([vt[rows], ones], axis=0), e_ref[h], preferred_element_type=F32)
        total = o[HEAD_DIM : HEAD_DIM + 1]
        weighted = jnp.sum(o[:HEAD_DIM] * gt[rows], axis=0, keepdims=True)
        for u in range(n):
            at = slice(u * (q.shape[0] // n), (u + 1) * (q.shape[0] // n))
            out_ref[col_ref[0] ^ u, 0, h : h + 1] = total[:, at]
            out_ref[col_ref[0] ^ u, 0, HEADS + h : HEADS + h + 1] = weighted[:, at]


def part_specs(part_len, bias, chunk):
    _, owners, _, step, width = bias.shape
    data = [pl.BlockSpec((2, 1, part_len, CH), lambda i, col: (0, i, 0, 0))] * 4
    return data + [
        pl.BlockSpec((1, owners, 1, step, width), lambda i, col, u=u: (col[0] ^ u, 0, chunk, 0, 0)) for u in range(4)
    ]


def totals(col, parts, bias, chunk, keys, values, key_gate):
    rows, key_len, _ = keys.shape
    part_len = parts[0].shape[2]
    n = len(parts)
    count = n * part_len
    per_row = lambda i, col: (i, 0, 0)
    work = rows * count * HEADS * key_len
    return pl.pallas_call(
        totals_kernel,
        grid_spec=pltpu.PrefetchScalarGridSpec(
            num_scalar_prefetch=1,
            grid=(rows,),
            in_specs=part_specs(part_len, bias, chunk)
            + [
                pl.BlockSpec((1, key_len, CH), per_row),
                pl.BlockSpec((1, key_len, CH), per_row),
                pl.BlockSpec((key_len, CH), lambda i, col: (0, 0)),
            ],
            out_specs=pl.BlockSpec((n, 1, 2 * HEADS, part_len), lambda i, col: (0, i, 0, 0)),
            scratch_shapes=[pltpu.VMEM((HEADS, key_len, count), BF16), pltpu.VMEM((HEADS, key_len, count), F32)],
        ),
        out_shape=jax.ShapeDtypeStruct((n, rows, 2 * HEADS, part_len), F32),
        compiler_params=pltpu.CompilerParams(vmem_limit_bytes=VMEM),
        cost_estimate=pl.CostEstimate(flops=work * 512 * 3, bytes_accessed=2**20, transcendentals=work),
        name="totals",
    )(col, *parts, *[bias] * n, keys, values, key_gate)


def split(x):
    a = x.astype(BF16)
    rest = x - a.astype(F32)
    b = rest.astype(BF16)
    return [y.astype(F32) for y in (a, b, (rest - b.astype(F32)).astype(BF16))]


def grads_kernel(first, last, col_ref, *refs):
    parts, biases, refs = refs[:4], refs[4:8], refs[8:]
    k_ref, v_ref, gate_ref, *refs = refs
    stats, refs = refs[:4], refs[4:]
    col = col_ref[0]
    if not first:
        dk_in, dv_in, *refs = refs
    dq_refs, refs = refs[:2], refs[2:]
    dk_out, dv_out, db_ref, kx_ref, vx_ref, sum_ref, p_ref, ds_ref, dk_ref, dv_ref, bias_ref = refs
    i = pl.program_id(0)
    q, g = joined(parts, 0), joined(parts, 1)
    count, key_len = q.shape[0], k_ref.shape[1]
    width = HEADS * key_len

    @pl.when(i == 0)
    def start():
        sum_ref[...] = jnp.zeros(sum_ref.shape, F32)
        bias_ref[...] = bias_block(biases) + jnp.concatenate([gate_ref[:1]] * HEADS, axis=1)
        lane = lax.broadcasted_iota(jnp.int32, (key_len, CH), 1)
        for h in range(HEADS):
            rows = slice(h * key_len, (h + 1) * key_len)
            for ref, at in ((kx_ref, h), (vx_ref, HEADS + h)):
                hit = (lane < 6 * HEADS) & (lane % (2 * HEADS) == at)
                ref[rows, CH:] = jnp.where(hit, -1.0, 0.0).astype(BF16)

    k, v = k_ref[0], v_ref[0]
    for h in range(HEADS):
        rows = slice(h * key_len, (h + 1) * key_len)
        kx_ref[rows, :CH] = only_head(k, h)
        vx_ref[rows, :CH] = only_head(v, h)

    stat = [sum(ref[col ^ u, 0] for ref in stats[1:]) + stats[0][col ^ u, 0] for u in range(4)]
    stat = jnp.concatenate(stat, axis=1)
    total = stat[:HEADS]
    level = jnp.log(total) * (1.0 / SCALE)
    delta = stat[HEADS:] / total
    pieces = split(jnp.concatenate([level, delta], axis=0))
    extra = jnp.concatenate(pieces + [jnp.zeros((CH - 6 * HEADS, count), F32)], axis=0).T.astype(BF16)
    qx = jnp.concatenate([q, extra], axis=1)
    gx = jnp.concatenate([g, extra], axis=1)
    qt, gt = q.T, g.T
    dq = jnp.zeros((count, CH), F32)
    for n in range(width // TILE):
        at = slice(n * TILE, (n + 1) * TILE)
        s = lax.dot_general(qx, kx_ref[at], NT, preferred_element_type=F32)
        t = lax.dot_general(gx, vx_ref[at], NT, preferred_element_type=F32)
        p = jnp.exp2(s * (SCALE * LOG2E) + bias_ref[:, at])
        ds = p * t
        sum_ref[:, at] += ds
        low = ds.astype(BF16)
        p_ref[:, at] = p.astype(BF16)
        ds_ref[:, at] = low
        dq = dq + jnp.dot(low, kx_ref[at, :CH], preferred_element_type=F32)
    dq = (dq * SCALE).astype(BF16)
    part_len = count // 4
    for u in range(4):
        dq_refs[u % 2][u // 2, 0] = dq[u * part_len : (u + 1) * part_len]
    for h in range(HEADS):
        rows, at = slice(h * HEAD_DIM, (h + 1) * HEAD_DIM), slice(h * key_len, (h + 1) * key_len)
        dv = jnp.dot(gt[rows], p_ref[:, at], preferred_element_type=F32)
        dk = jnp.dot(qt[rows], ds_ref[:, at], preferred_element_type=F32)
        if not first:
            dv, dk = dv + dv_in[0, rows], dk + dk_in[0, rows]
        if last:
            dv_ref[rows] = dv
            dk_ref[rows] = dk * SCALE
        else:
            dv_out[0, rows] = dv
            dk_out[0, rows] = dk
    if last:
        dv_out[0] = dv_ref[...].T.astype(BF16)
        dk_out[0] = dk_ref[...].T.astype(BF16)

    @pl.when(i == pl.num_programs(0) - 1)
    def finish():
        for u in range(4):
            part = sum_ref[u * part_len : (u + 1) * part_len].astype(BF16)
            db_ref[col ^ u] = part.reshape(db_ref.shape[1:])


def grads(col, parts, bias, chunk, keys, values, row_gate, stats, carried, last):
    rows, key_len, _ = keys.shape
    part_len = parts[0].shape[2]
    count, width = 4 * part_len, HEADS * key_len
    per_row = lambda i, col: (i, 0, 0)
    whole = lambda i, col: (0, 0)
    share = (bias.shape[1], bias.shape[3], width)
    side = pl.BlockSpec((1, CH, key_len), per_row)
    side_shape = jax.ShapeDtypeStruct((rows, CH, key_len), F32)
    final = pl.BlockSpec((1, key_len, CH), per_row)
    final_shape = jax.ShapeDtypeStruct((rows, key_len, CH), BF16)
    work = rows * count * width
    return pl.pallas_call(
        functools.partial(grads_kernel, not carried, last),
        grid_spec=pltpu.PrefetchScalarGridSpec(
            num_scalar_prefetch=1,
            grid=(rows,),
            in_specs=part_specs(part_len, bias, chunk)
            + [
                pl.BlockSpec((1, key_len, CH), per_row),
                pl.BlockSpec((1, key_len, CH), per_row),
                pl.BlockSpec((8, key_len), whole),
            ]
            + [pl.BlockSpec((4, 1, 2 * HEADS, part_len), lambda i, col: (0, i, 0, 0))] * 4
            + [side] * len(carried),
            out_specs=[
                *[pl.BlockSpec((2, 1, part_len, CH), lambda i, col: (0, i, 0, 0))] * 2,
                final if last else side,
                final if last else side,
                pl.BlockSpec((4,) + share, lambda i, col: (0, 0, 0, 0)),
            ],
            scratch_shapes=[
                pltpu.VMEM((width, 2 * CH), BF16),
                pltpu.VMEM((width, 2 * CH), BF16),
                pltpu.VMEM((count, width), F32),
                pltpu.VMEM((count, width), BF16),
                pltpu.VMEM((count, width), BF16),
                pltpu.VMEM((CH, key_len), F32),
                pltpu.VMEM((CH, key_len), F32),
                pltpu.VMEM((count, width), F32),
            ],
        ),
        out_shape=[
            *[jax.ShapeDtypeStruct((2, rows, part_len, CH), BF16)] * 2,
            final_shape if last else side_shape,
            final_shape if last else side_shape,
            jax.ShapeDtypeStruct((4,) + share, BF16),
        ],
        compiler_params=pltpu.CompilerParams(vmem_limit_bytes=VMEM),
        cost_estimate=pl.CostEstimate(flops=work * 512 * 6, bytes_accessed=2**20, transcendentals=work),
        name="grads",
    )(col, *parts, *[bias] * 4, keys, values, row_gate, *stats, *carried)


def partner(x, distance):
    return lax.ppermute(x, "cols", [(c, c ^ distance) for c in range(4)])


def per_device(queries, keys, values, out_grad, pair_bias, token_mask, span_index):
    rows, key_len, _ = keys.shape
    col = lax.axis_index("cols")
    owners = 8
    span = key_len // owners
    step = span // CHUNKS
    part_len = owners * step
    count = 4 * part_len
    width = HEADS * key_len

    row_keep = lax.dynamic_slice_in_dim(token_mask, span_index[0] * rows, rows)
    masked = out_grad * row_keep.astype(BF16)[:, None, None]
    pairs = jnp.stack([queries, masked]).reshape(2, rows, owners, CHUNKS, step, CH)

    key_keep = lax.dynamic_slice_in_dim(token_mask, col * key_len, key_len) > 0
    gate = jnp.where(key_keep, F32(0.0), F32(-1e30))
    key_gate = jnp.broadcast_to(gate[:, None], (key_len, CH))
    row_gate = jnp.broadcast_to(gate[None, :], (8, key_len))
    bias = jnp.concatenate([pair_bias[:, h] for h in range(HEADS)], axis=1).reshape(4, owners, CHUNKS, step, width)
    col_id = col.astype(jnp.int32).reshape(1)

    tie = lax.optimization_barrier
    owns = [pairs[:, :, :, b].reshape(2, rows, part_len, CH) for b in range(CHUNKS)]

    def spread(own, far):
        return [own, partner(own, 1), far, partner(far, 1)]

    def call_totals(b):
        return totals(col_id, parts[b], bias, b, keys, values, key_gate)

    def all_stats(stat):
        return [stat] + [partner(stat, distance) for distance in (1, 2, 3)]

    def call_grads(b, stats, carried):
        *dq, dk, dv, db = grads(
            col_id, parts[b], bias, b, keys, values, row_gate, stats, carried, b == CHUNKS - 1
        )
        return dq, (dk, dv), db.reshape(32, step, width)

    def near_queries(dq):
        pair = dq[0].astype(F32) + partner(dq[1], 1).astype(F32)
        return pair[0], pair[1].astype(BF16)

    def far_queries(pair):
        return (pair[0] + partner(pair[1], 2).astype(F32)).astype(BF16)

    def swap_bias(db):
        return lax.all_to_all(db, "rows", 0, 0, tiled=True)

    def summed(terms):
        return jnp.sum(terms.astype(F32), axis=0)

    far0, bias = tie((partner(owns[0], 2), bias))
    far0, owns[1] = tie((far0, owns[1]))
    far1 = partner(owns[1], 2)
    parts = [spread(owns[0], far0), None, None]
    t0 = call_totals(0)
    far1, owns[2], t0 = tie((far1, owns[2], t0))
    far2 = partner(owns[2], 2)
    parts[1] = spread(owns[1], far1)
    t1 = call_totals(1)
    far2, t1, s0 = tie((far2, t1, all_stats(t0)))
    parts[2] = spread(owns[2], far2)
    t2 = call_totals(2)
    t2, s0, s1 = tie((t2, s0, all_stats(t1)))
    dq0, carried, db0 = call_grads(0, s0, ())
    dq0, db0, s1, s2 = tie((dq0, db0, s1, all_stats(t2)))
    dq1, carried, db1 = call_grads(1, s1, carried)
    n0, db0, dq1, db1 = tie((near_queries(dq0), swap_bias(db0), dq1, db1))
    dq2, carried, db2 = call_grads(2, s2, carried)
    q0, n1, db1, dq2, db2 = tie((far_queries(n0), near_queries(dq1), swap_bias(db1), dq2, db2))
    n2, db2 = tie((near_queries(dq2), db2))
    db2 = swap_bias(db2)
    q1, q2 = far_queries(n1), far_queries(n2)
    b0, b1, b2 = [summed(db) for db in (db0, db1, db2)]
    key_grad, value_grad = carried
    query_grad = jnp.stack([q0, q1, q2]).reshape(CHUNKS, rows, owners, step, CH)
    query_grad = query_grad.transpose(1, 2, 0, 3, 4).reshape(rows, key_len, CH)
    bias_grad = jnp.concatenate([b0, b1, b2], axis=0).reshape(span, HEADS, key_len)
    return (query_grad, key_grad, value_grad, bias_grad)


def solution(mesh):
    return jax.shard_map(
        per_device,
        mesh=mesh,
        in_specs=(
            P("rows", "cols", None),
            P("rows", "cols", None),
            P("rows", "cols", None),
            P("rows", "cols", None),
            P(None, None, "cols"),
            P(),
            P("rows"),
        ),
        out_specs=(
            P("rows", "cols", None),
            P("rows", "cols", None),
            P("rows", "cols", None),
            P("rows", None, "cols"),
        ),
        check_vma=False,
    )
```

```python
import functools

import jax
import jax.numpy as jnp
from jax import lax
from jax.experimental import pallas as pl
from jax.experimental.pallas import tpu as pltpu
from jax.sharding import PartitionSpec as P

HEADS = 4
HEAD_DIM = 32
CH = HEADS * HEAD_DIM
SCALE = HEAD_DIM**-0.5
LOG2E = 1.4426950408889634
CHUNKS = 2
TILE = 256
VMEM = 60 * 2**20
NT = (((1,), (1,)), ((), ()))
F32 = jnp.float32
BF16 = jnp.bfloat16


def only_head(x, h):
    lane = lax.broadcasted_iota(jnp.int32, (1, x.shape[1]), 1)
    hit = (lane >= h * HEAD_DIM) & (lane < (h + 1) * HEAD_DIM)
    return x * jnp.where(hit, 1.0, 0.0).astype(BF16)


def joined(parts, which):
    return jnp.concatenate([part[which, 0] for part in parts], axis=0)


def bias_block(parts):
    return jnp.concatenate([part[0, 0] for part in parts], axis=0).astype(F32) * LOG2E


def totals_kernel(col_ref, *refs):
    n = (len(refs) - 6) // 2
    parts, biases, (k_ref, v_ref, gate_ref, out_ref, e_ref, bias_ref) = refs[:n], refs[n : 2 * n], refs[2 * n :]
    q, g = joined(parts, 0), joined(parts, 1)
    k = k_ref[0]
    key_len = k.shape[0]

    @pl.when(pl.program_id(0) == 0)
    def start():
        bias = bias_block(biases)
        gate = jnp.concatenate([gate_ref[...]] * (q.shape[0] // CH), axis=1)
        for h in range(HEADS):
            bias_ref[h] = bias[:, h * key_len : (h + 1) * key_len].T + gate

    for h in range(HEADS):
        s = lax.dot_general(k, only_head(q, h), NT, preferred_element_type=F32)
        e_ref[h] = jnp.exp2(s * (SCALE * LOG2E) + bias_ref[h]).astype(BF16)
    gt = g.T.astype(F32)
    vt = v_ref[0].T
    ones = jnp.ones((16, key_len), BF16)
    for h in range(HEADS):
        rows = slice(h * HEAD_DIM, (h + 1) * HEAD_DIM)
        o = jnp.dot(jnp.concatenate([vt[rows], ones], axis=0), e_ref[h], preferred_element_type=F32)
        total = o[HEAD_DIM : HEAD_DIM + 1]
        weighted = jnp.sum(o[:HEAD_DIM] * gt[rows], axis=0, keepdims=True)
        for u in range(n):
            at = slice(u * (q.shape[0] // n), (u + 1) * (q.shape[0] // n))
            out_ref[col_ref[0] ^ u, 0, h : h + 1] = total[:, at]
            out_ref[col_ref[0] ^ u, 0, HEADS + h : HEADS + h + 1] = weighted[:, at]


def part_specs(part_len, bias, chunk):
    width = bias.shape[-1]
    data = [pl.BlockSpec((2, 1, part_len, CH), lambda i, col: (0, i, 0, 0))] * 4
    return data + [
        pl.BlockSpec((1, 1, part_len, width), lambda i, col, u=u: (chunk, col[0] ^ u, 0, 0)) for u in range(4)
    ]


def totals(col, parts, bias, chunk, keys, values, key_gate):
    rows, key_len, _ = keys.shape
    part_len = parts[0].shape[2]
    n = len(parts)
    count = n * part_len
    per_row = lambda i, col: (i, 0, 0)
    work = rows * count * HEADS * key_len
    return pl.pallas_call(
        totals_kernel,
        grid_spec=pltpu.PrefetchScalarGridSpec(
            num_scalar_prefetch=1,
            grid=(rows,),
            in_specs=part_specs(part_len, bias, chunk)
            + [
                pl.BlockSpec((1, key_len, CH), per_row),
                pl.BlockSpec((1, key_len, CH), per_row),
                pl.BlockSpec((key_len, CH), lambda i, col: (0, 0)),
            ],
            out_specs=pl.BlockSpec((n, 1, 2 * HEADS, part_len), lambda i, col: (0, i, 0, 0)),
            scratch_shapes=[pltpu.VMEM((HEADS, key_len, count), BF16), pltpu.VMEM((HEADS, key_len, count), F32)],
        ),
        out_shape=jax.ShapeDtypeStruct((n, rows, 2 * HEADS, part_len), F32),
        compiler_params=pltpu.CompilerParams(vmem_limit_bytes=VMEM),
        cost_estimate=pl.CostEstimate(flops=work * 512 * 3, bytes_accessed=2**20, transcendentals=work),
        name="totals",
    )(col, *parts, *[bias] * n, keys, values, key_gate)


def split(x):
    a = x.astype(BF16)
    rest = x - a.astype(F32)
    b = rest.astype(BF16)
    return [y.astype(F32) for y in (a, b, (rest - b.astype(F32)).astype(BF16))]


def load_keys(ref, x, column=None):
    key_len = x.shape[0]
    for h in range(HEADS):
        rows = slice(h * key_len, (h + 1) * key_len)
        if column is None:
            ref[rows, :CH] = only_head(x, h)
        else:
            lane = lax.broadcasted_iota(jnp.int32, (key_len, CH), 1)
            hit = (lane < 6 * HEADS) & (lane % (2 * HEADS) == column + h)
            ref[rows, CH:] = jnp.where(hit, -1.0, 0.0).astype(BF16)


def with_extra(q, g, stats, col):
    stat = [sum(ref[col ^ u, 0] for ref in stats[1:]) + stats[0][col ^ u, 0] for u in range(4)]
    stat = jnp.concatenate(stat, axis=1)
    total = stat[:HEADS]
    level = jnp.log(total) * (1.0 / SCALE)
    delta = stat[HEADS:] / total
    pieces = split(jnp.concatenate([level, delta], axis=0))
    extra = jnp.concatenate(pieces + [jnp.zeros((CH - 6 * HEADS, q.shape[0]), F32)], axis=0).T.astype(BF16)
    return jnp.concatenate([q, extra], axis=1), jnp.concatenate([g, extra], axis=1)


def chances(qx, gx, kx_ref, vx_ref, bias_ref, at):
    s = lax.dot_general(qx, kx_ref[at], NT, preferred_element_type=F32)
    t = lax.dot_general(gx, vx_ref[at], NT, preferred_element_type=F32)
    p = jnp.exp2(s * (SCALE * LOG2E) + bias_ref[:, at])
    return p, p * t


def prepare(biases, gate_ref, sum_ref, bias_ref, kx_ref, vx_ref, k, v):
    @pl.when(pl.program_id(0) == 0)
    def start():
        sum_ref[...] = jnp.zeros(sum_ref.shape, F32)
        bias_ref[...] = bias_block(biases) + jnp.concatenate([gate_ref[:1]] * HEADS, axis=1)
        load_keys(kx_ref, k, 0)
        load_keys(vx_ref, v, HEADS)

    load_keys(kx_ref, k)
    load_keys(vx_ref, v)


def store_bias(col, sum_ref, db_ref):
    @pl.when(pl.program_id(0) == pl.num_programs(0) - 1)
    def finish():
        part_len = db_ref.shape[1]
        for u in range(4):
            db_ref[col ^ u] = sum_ref[u * part_len : (u + 1) * part_len].astype(BF16)


def store_queries(dq, dq_refs):
    dq = (dq * SCALE).astype(BF16)
    part_len = dq.shape[0] // 4
    for u in range(4):
        dq_refs[u % 2][u // 2, 0] = dq[u * part_len : (u + 1) * part_len]


def grads_kernel(col_ref, *refs):
    parts, biases, refs = refs[:4], refs[4:8], refs[8:]
    k_ref, v_ref, gate_ref, *refs = refs
    stats, dq_refs, refs = refs[:4], refs[4:6], refs[6:]
    dk_ref, dv_ref, db_ref, kx_ref, vx_ref, sum_ref, p_ref, ds_ref, bias_ref = refs
    col = col_ref[0]
    q, g = joined(parts, 0), joined(parts, 1)
    key_len = k_ref.shape[1]
    prepare(biases, gate_ref, sum_ref, bias_ref, kx_ref, vx_ref, k_ref[0], v_ref[0])
    qx, gx = with_extra(q, g, stats, col)
    qt, gt = q.T, g.T
    dq = jnp.zeros((q.shape[0], CH), F32)
    for n in range(HEADS * key_len // TILE):
        at = slice(n * TILE, (n + 1) * TILE)
        p, ds = chances(qx, gx, kx_ref, vx_ref, bias_ref, at)
        sum_ref[:, at] += ds
        low = ds.astype(BF16)
        p_ref[:, at] = p.astype(BF16)
        ds_ref[:, at] = low
        dq = dq + jnp.dot(low, kx_ref[at, :CH], preferred_element_type=F32)
    store_queries(dq, dq_refs)
    for h in range(HEADS):
        rows, at = slice(h * HEAD_DIM, (h + 1) * HEAD_DIM), slice(h * key_len, (h + 1) * key_len)
        dv_ref[0, rows] = jnp.dot(gt[rows], p_ref[:, at], preferred_element_type=F32)
        dk_ref[0, rows] = jnp.dot(qt[rows], ds_ref[:, at], preferred_element_type=F32)
    store_bias(col, sum_ref, db_ref)


def chances_kernel(col_ref, *refs):
    parts, biases, refs = refs[:4], refs[4:8], refs[8:]
    k_ref, v_ref, gate_ref, *refs = refs
    stats, refs = refs[:4], refs[4:]
    p_ref, ds_ref, db_ref, kx_ref, vx_ref, sum_ref, bias_ref = refs
    col = col_ref[0]
    prepare(biases, gate_ref, sum_ref, bias_ref, kx_ref, vx_ref, k_ref[0], v_ref[0])
    qx, gx = with_extra(joined(parts, 0), joined(parts, 1), stats, col)
    for n in range(HEADS * k_ref.shape[1] // TILE):
        at = slice(n * TILE, (n + 1) * TILE)
        p, ds = chances(qx, gx, kx_ref, vx_ref, bias_ref, at)
        sum_ref[:, at] += ds
        p_ref[0, :, at] = p.astype(BF16)
        ds_ref[0, :, at] = ds.astype(BF16)
    store_bias(col, sum_ref, db_ref)


def products_kernel(*refs):
    parts, refs = refs[:4], refs[4:]
    k_ref, p_ref, ds_ref, dk_in, dv_in, *refs = refs
    dq_refs, (dk_out, dv_out, kx_ref, dk_ref, dv_ref) = refs[:2], refs[2:]
    q, g = joined(parts, 0), joined(parts, 1)
    key_len = k_ref.shape[1]
    load_keys(kx_ref, k_ref[0])
    store_queries(jnp.dot(ds_ref[0], kx_ref[...], preferred_element_type=F32), dq_refs)
    qt, gt = q.T, g.T
    for h in range(HEADS):
        rows, at = slice(h * HEAD_DIM, (h + 1) * HEAD_DIM), slice(h * key_len, (h + 1) * key_len)
        dv_ref[rows] = jnp.dot(gt[rows], p_ref[0, :, at], preferred_element_type=F32) + dv_in[0, rows]
        dk = jnp.dot(qt[rows], ds_ref[0, :, at], preferred_element_type=F32)
        dk_ref[rows] = (dk + dk_in[0, rows]) * SCALE
    dv_out[0] = dv_ref[...].T.astype(BF16)
    dk_out[0] = dk_ref[...].T.astype(BF16)


def grads(kind, col, parts, bias, chunk, keys, values, row_gate, stats, carried=()):
    rows, key_len, _ = keys.shape
    part_len = parts[0].shape[2]
    count, width = 4 * part_len, HEADS * key_len
    per_row = lambda i, *col: (i, 0, 0)
    whole = lambda i, *col: (0, 0)
    data = pl.BlockSpec((1, key_len, CH), per_row)
    side = pl.BlockSpec((1, CH, key_len), per_row)
    side_shape = jax.ShapeDtypeStruct((rows, CH, key_len), F32)
    data_shape = jax.ShapeDtypeStruct(keys.shape, BF16)
    square = pl.BlockSpec((1, count, width), per_row)
    square_shape = jax.ShapeDtypeStruct((rows, count, width), BF16)
    dq_specs = [pl.BlockSpec((2, 1, part_len, CH), lambda i, *col: (0, i, 0, 0))] * 2
    dq_shapes = [jax.ShapeDtypeStruct((2, rows, part_len, CH), BF16)] * 2
    db_spec = pl.BlockSpec((4, part_len, width), lambda i, *col: (0, 0, 0))
    db_shape = jax.ShapeDtypeStruct((4, part_len, width), BF16)
    stat_specs = [pl.BlockSpec((4, 1, 2 * HEADS, part_len), lambda i, col: (0, i, 0, 0))] * 4
    keys_scratch = pltpu.VMEM((width, 2 * CH), BF16)
    wide, low = pltpu.VMEM((count, width), F32), pltpu.VMEM((count, width), BF16)
    flops = rows * count * width * 512
    if kind == "products":
        return pl.pallas_call(
            products_kernel,
            grid=(rows,),
            in_specs=[pl.BlockSpec((2, 1, part_len, CH), lambda i: (0, i, 0, 0))] * 4
            + [data, square, square, side, side],
            out_specs=dq_specs + [data, data],
            out_shape=dq_shapes + [data_shape, data_shape],
            scratch_shapes=[pltpu.VMEM((width, CH), BF16), pltpu.VMEM((CH, key_len), F32), pltpu.VMEM((CH, key_len), F32)],
            compiler_params=pltpu.CompilerParams(vmem_limit_bytes=VMEM),
            cost_estimate=pl.CostEstimate(flops=flops * 3, bytes_accessed=2**20, transcendentals=0),
            name="products",
        )(*parts, keys, *carried)
    in_specs = part_specs(part_len, bias, chunk) + [data, data, pl.BlockSpec((8, key_len), whole)] + stat_specs
    if kind == "chances":
        out_specs, out_shape = [square, square, db_spec], [square_shape, square_shape, db_shape]
        scratch = [keys_scratch, keys_scratch, wide, wide]
    else:
        out_specs = dq_specs + [side, side, db_spec]
        out_shape = dq_shapes + [side_shape, side_shape, db_shape]
        scratch = [keys_scratch, keys_scratch, wide, low, low, wide]
    return pl.pallas_call(
        chances_kernel if kind == "chances" else grads_kernel,
        grid_spec=pltpu.PrefetchScalarGridSpec(
            num_scalar_prefetch=1, grid=(rows,), in_specs=in_specs, out_specs=out_specs, scratch_shapes=scratch
        ),
        out_shape=out_shape,
        compiler_params=pltpu.CompilerParams(vmem_limit_bytes=VMEM),
        cost_estimate=pl.CostEstimate(flops=flops * (4 if kind == "chances" else 6), bytes_accessed=2**20, transcendentals=0),
        name=kind,
    )(col, *parts, *[bias] * 4, keys, values, row_gate, *stats)


def partner(x, distance):
    return lax.ppermute(x, "cols", [(c, c ^ distance) for c in range(4)])


def per_device(queries, keys, values, out_grad, pair_bias, token_mask, span_index):
    rows, key_len, _ = keys.shape
    col = lax.axis_index("cols")
    owners = 8
    span = key_len // owners
    step = span // CHUNKS
    part_len = owners * step
    count = 4 * part_len
    width = HEADS * key_len

    row_keep = lax.dynamic_slice_in_dim(token_mask, span_index[0] * rows, rows)
    masked = out_grad * row_keep.astype(BF16)[:, None, None]
    pairs = jnp.stack([queries, masked]).reshape(2, rows, owners, CHUNKS, step, CH)

    key_keep = lax.dynamic_slice_in_dim(token_mask, col * key_len, key_len) > 0
    gate = jnp.where(key_keep, F32(0.0), F32(-1e30))
    key_gate = jnp.broadcast_to(gate[:, None], (key_len, CH))
    row_gate = jnp.broadcast_to(gate[None, :], (8, key_len))
    bias = jnp.concatenate([pair_bias[:, h] for h in range(HEADS)], axis=1)
    bias = bias.reshape(4 * owners, CHUNKS, step, width).swapaxes(0, 1).reshape(CHUNKS, 4, part_len, width)
    col_id = col.astype(jnp.int32).reshape(1)

    tie = lax.optimization_barrier
    owns = [pairs[:, :, :, b].reshape(2, rows, part_len, CH) for b in range(CHUNKS)]

    def spread(own, far):
        return [own, partner(own, 1), far, partner(far, 1)]

    def call_totals(b):
        return totals(col_id, parts[b], bias, b, keys, values, key_gate)

    def all_stats(stat):
        return [stat] + [partner(stat, distance) for distance in (1, 2, 3)]

    def call_grads(kind, b, stats, carried=()):
        return grads(kind, col_id, parts[b], bias, b, keys, values, row_gate, stats, carried)

    def near_queries(dq):
        pair = dq[0].astype(F32) + partner(dq[1], 1).astype(F32)
        return pair[0], pair[1].astype(BF16)

    def far_queries(pair):
        return (pair[0] + partner(pair[1], 2).astype(F32)).astype(BF16)

    def swap_bias(db):
        return lax.all_to_all(db.reshape(32, step, width), "rows", 0, 0, tiled=True)

    def summed(terms):
        return jnp.sum(terms.astype(F32), axis=0)

    far0, bias = tie((partner(owns[0], 2), bias))
    far0, owns[1] = tie((far0, owns[1]))
    far1 = partner(owns[1], 2)
    parts = [spread(owns[0], far0), None]
    t0 = call_totals(0)
    far1, t0 = tie((far1, t0))
    parts[1] = spread(owns[1], far1)
    t1 = call_totals(1)
    s0, t1 = tie((all_stats(t0), t1))
    p, ds, db0 = call_grads("chances", 0, s0)
    db0, s1 = tie((db0, all_stats(t1)))
    *dq1, dk, dv, db1 = call_grads("grads", 1, s1)
    db0, dq1, db1 = tie((swap_bias(db0), dq1, db1))
    db1 = swap_bias(db1)
    n1, p = tie((near_queries(dq1), p))
    *dq0, key_grad, value_grad = call_grads("products", 0, (), (p, ds, dk, dv))
    q1, dq0 = tie((far_queries(n1), dq0))
    n0 = near_queries(dq0)
    queries_out = [far_queries(n0), q1]
    bias_out = [summed(db0), summed(db1)]
    query_grad = jnp.stack(queries_out).reshape(CHUNKS, rows, owners, step, CH)
    query_grad = query_grad.transpose(1, 2, 0, 3, 4).reshape(rows, key_len, CH)
    bias_grad = jnp.concatenate(bias_out, axis=0).reshape(span, HEADS, key_len)
    return (query_grad, key_grad, value_grad, bias_grad)


def solution(mesh):
    return jax.shard_map(
        per_device,
        mesh=mesh,
        in_specs=(
            P("rows", "cols", None),
            P("rows", "cols", None),
            P("rows", "cols", None),
            P("rows", "cols", None),
            P(None, None, "cols"),
            P(),
            P("rows"),
        ),
        out_specs=(
            P("rows", "cols", None),
            P("rows", "cols", None),
            P("rows", "cols", None),
            P("rows", None, "cols"),
        ),
        check_vma=False,
    )
```

```python
import functools

import jax
import jax.numpy as jnp
from jax import lax
from jax.experimental import pallas as pl
from jax.experimental.pallas import tpu as pltpu
from jax.sharding import PartitionSpec as P

HEADS = 4
HEAD_DIM = 32
CH = HEADS * HEAD_DIM
SCALE = HEAD_DIM**-0.5
LOG2E = 1.4426950408889634
CHUNKS = 2
TILE = 256
VMEM = 60 * 2**20
NT = (((1,), (1,)), ((), ()))
F32 = jnp.float32
BF16 = jnp.bfloat16


def only_head(x, h):
    lane = lax.broadcasted_iota(jnp.int32, (1, x.shape[1]), 1)
    hit = (lane >= h * HEAD_DIM) & (lane < (h + 1) * HEAD_DIM)
    return x * jnp.where(hit, 1.0, 0.0).astype(BF16)


def joined(parts, which):
    return jnp.concatenate([part[which, 0] for part in parts], axis=0)


def bias_block(parts):
    return jnp.concatenate([part[0, 0] for part in parts], axis=0).astype(F32) * LOG2E


def totals_kernel(col_ref, *refs):
    n = (len(refs) - 6) // 2
    parts, biases, (k_ref, v_ref, gate_ref, out_ref, e_ref, bias_ref) = refs[:n], refs[n : 2 * n], refs[2 * n :]
    q, g = joined(parts, 0), joined(parts, 1)
    k = k_ref[0]
    key_len = k.shape[0]

    @pl.when(pl.program_id(0) == 0)
    def start():
        bias = bias_block(biases)
        gate = jnp.concatenate([gate_ref[...]] * (q.shape[0] // CH), axis=1)
        for h in range(HEADS):
            bias_ref[h] = bias[:, h * key_len : (h + 1) * key_len].T + gate

    for h in range(HEADS):
        s = lax.dot_general(k, only_head(q, h), NT, preferred_element_type=F32)
        e_ref[h] = jnp.exp2(s * (SCALE * LOG2E) + bias_ref[h]).astype(BF16)
    gt = g.T.astype(F32)
    vt = v_ref[0].T
    ones = jnp.ones((16, key_len), BF16)
    for h in range(HEADS):
        rows = slice(h * HEAD_DIM, (h + 1) * HEAD_DIM)
        o = jnp.dot(jnp.concatenate([vt[rows], ones], axis=0), e_ref[h], preferred_element_type=F32)
        total = o[HEAD_DIM : HEAD_DIM + 1]
        weighted = jnp.sum(o[:HEAD_DIM] * gt[rows], axis=0, keepdims=True)
        for u in range(n):
            at = slice(u * (q.shape[0] // n), (u + 1) * (q.shape[0] // n))
            out_ref[col_ref[0] ^ u, 0, h : h + 1] = total[:, at]
            out_ref[col_ref[0] ^ u, 0, HEADS + h : HEADS + h + 1] = weighted[:, at]


def part_specs(part_len, bias, chunk):
    width = bias.shape[-1]
    data = [pl.BlockSpec((2, 1, part_len, CH), lambda i, col: (0, i, 0, 0))] * 4
    return data + [
        pl.BlockSpec((1, 1, part_len, width), lambda i, col, u=u: (chunk, col[0] ^ u, 0, 0)) for u in range(4)
    ]


def totals(col, parts, bias, chunk, keys, values, key_gate):
    rows, key_len, _ = keys.shape
    part_len = parts[0].shape[2]
    n = len(parts)
    count = n * part_len
    per_row = lambda i, col: (i, 0, 0)
    work = rows * count * HEADS * key_len
    return pl.pallas_call(
        totals_kernel,
        grid_spec=pltpu.PrefetchScalarGridSpec(
            num_scalar_prefetch=1,
            grid=(rows,),
            in_specs=part_specs(part_len, bias, chunk)
            + [
                pl.BlockSpec((1, key_len, CH), per_row),
                pl.BlockSpec((1, key_len, CH), per_row),
                pl.BlockSpec((key_len, CH), lambda i, col: (0, 0)),
            ],
            out_specs=pl.BlockSpec((n, 1, 2 * HEADS, part_len), lambda i, col: (0, i, 0, 0)),
            scratch_shapes=[pltpu.VMEM((HEADS, key_len, count), BF16), pltpu.VMEM((HEADS, key_len, count), F32)],
        ),
        out_shape=jax.ShapeDtypeStruct((n, rows, 2 * HEADS, part_len), F32),
        compiler_params=pltpu.CompilerParams(vmem_limit_bytes=VMEM),
        cost_estimate=pl.CostEstimate(flops=work * 512 * 3, bytes_accessed=2**20, transcendentals=work),
        name="totals",
    )(col, *parts, *[bias] * n, keys, values, key_gate)


def split(x):
    a = x.astype(BF16)
    rest = x - a.astype(F32)
    b = rest.astype(BF16)
    return [y.astype(F32) for y in (a, b, (rest - b.astype(F32)).astype(BF16))]


def load_keys(ref, x, column=None):
    key_len = x.shape[0]
    for h in range(HEADS):
        rows = slice(h * key_len, (h + 1) * key_len)
        if column is None:
            ref[rows, :CH] = only_head(x, h)
        else:
            lane = lax.broadcasted_iota(jnp.int32, (key_len, CH), 1)
            hit = (lane < 6 * HEADS) & (lane % (2 * HEADS) == column + h)
            ref[rows, CH:] = jnp.where(hit, -1.0, 0.0).astype(BF16)


def with_extra(q, g, stats, col):
    stat = [sum(ref[col ^ u, 0] for ref in stats[1:]) + stats[0][col ^ u, 0] for u in range(4)]
    stat = jnp.concatenate(stat, axis=1)
    total = stat[:HEADS]
    level = jnp.log(total) * (1.0 / SCALE)
    delta = stat[HEADS:] / total
    pieces = split(jnp.concatenate([level, delta], axis=0))
    extra = jnp.concatenate(pieces + [jnp.zeros((CH - 6 * HEADS, q.shape[0]), F32)], axis=0).T.astype(BF16)
    return jnp.concatenate([q, extra], axis=1), jnp.concatenate([g, extra], axis=1)


def chances(qx, gx, kx_ref, vx_ref, bias_ref, at):
    s = lax.dot_general(qx, kx_ref[at], NT, preferred_element_type=F32)
    t = lax.dot_general(gx, vx_ref[at], NT, preferred_element_type=F32)
    p = jnp.exp2(s * (SCALE * LOG2E) + bias_ref[:, at])
    return p, p * t


def prepare(biases, gate_ref, sum_ref, bias_ref, kx_ref, vx_ref, k, v):
    @pl.when(pl.program_id(0) == 0)
    def start():
        sum_ref[...] = jnp.zeros(sum_ref.shape, F32)
        bias_ref[...] = bias_block(biases) + jnp.concatenate([gate_ref[:1]] * HEADS, axis=1)
        load_keys(kx_ref, k, 0)
        load_keys(vx_ref, v, HEADS)

    load_keys(kx_ref, k)
    load_keys(vx_ref, v)


def store_bias(col, sum_ref, db_ref):
    @pl.when(pl.program_id(0) == pl.num_programs(0) - 1)
    def finish():
        part_len = db_ref.shape[1]
        for u in range(4):
            db_ref[col ^ u] = sum_ref[u * part_len : (u + 1) * part_len].astype(BF16)


def store_queries(dq, dq_refs):
    dq = (dq * SCALE).astype(BF16)
    part_len = dq.shape[0] // 4
    for u in range(4):
        dq_refs[u % 2][u // 2, 0] = dq[u * part_len : (u + 1) * part_len]


def grads_kernel(col_ref, *refs):
    parts, biases, refs = refs[:4], refs[4:8], refs[8:]
    k_ref, v_ref, gate_ref, *refs = refs
    stats, dq_refs, refs = refs[:4], refs[4:6], refs[6:]
    dk_ref, dv_ref, db_ref, kx_ref, vx_ref, sum_ref, p_ref, ds_ref, bias_ref = refs
    col = col_ref[0]
    q, g = joined(parts, 0), joined(parts, 1)
    key_len = k_ref.shape[1]
    prepare(biases, gate_ref, sum_ref, bias_ref, kx_ref, vx_ref, k_ref[0], v_ref[0])
    qx, gx = with_extra(q, g, stats, col)
    qt, gt = q.T, g.T
    dq = jnp.zeros((q.shape[0], CH), F32)
    for n in range(HEADS * key_len // TILE):
        at = slice(n * TILE, (n + 1) * TILE)
        p, ds = chances(qx, gx, kx_ref, vx_ref, bias_ref, at)
        sum_ref[:, at] += ds
        low = ds.astype(BF16)
        p_ref[:, at] = p.astype(BF16)
        ds_ref[:, at] = low
        dq = dq + jnp.dot(low, kx_ref[at, :CH], preferred_element_type=F32)
    store_queries(dq, dq_refs)
    for h in range(HEADS):
        rows, at = slice(h * HEAD_DIM, (h + 1) * HEAD_DIM), slice(h * key_len, (h + 1) * key_len)
        dv_ref[0, rows] = jnp.dot(gt[rows], p_ref[:, at], preferred_element_type=F32)
        dk_ref[0, rows] = jnp.dot(qt[rows], ds_ref[:, at], preferred_element_type=F32)
    store_bias(col, sum_ref, db_ref)


def chances_kernel(col_ref, *refs):
    parts, biases, refs = refs[:4], refs[4:8], refs[8:]
    k_ref, v_ref, gate_ref, *refs = refs
    stats, refs = refs[:4], refs[4:]
    dv_ref, ds_ref, db_ref, kx_ref, vx_ref, sum_ref, bias_ref, p_ref = refs
    col = col_ref[0]
    prepare(biases, gate_ref, sum_ref, bias_ref, kx_ref, vx_ref, k_ref[0], v_ref[0])
    qx, gx = with_extra(joined(parts, 0), joined(parts, 1), stats, col)
    for n in range(HEADS * k_ref.shape[1] // TILE):
        at = slice(n * TILE, (n + 1) * TILE)
        p, ds = chances(qx, gx, kx_ref, vx_ref, bias_ref, at)
        sum_ref[:, at] += ds
        p_ref[:, at] = p.astype(BF16)
        ds_ref[0, :, at] = ds.astype(BF16)
    gt, key_len = joined(parts, 1).T, k_ref.shape[1]
    for h in range(HEADS):
        rows, at = slice(h * HEAD_DIM, (h + 1) * HEAD_DIM), slice(h * key_len, (h + 1) * key_len)
        dv_ref[0, rows] = jnp.dot(gt[rows], p_ref[:, at], preferred_element_type=F32)
    store_bias(col, sum_ref, db_ref)


def products_kernel(*refs):
    parts, refs = refs[:4], refs[4:]
    k_ref, dv_first, ds_ref, dk_in, dv_in, *refs = refs
    dq_refs, (dk_out, dv_out, kx_ref, dk_ref, dv_ref) = refs[:2], refs[2:]
    q, g = joined(parts, 0), joined(parts, 1)
    key_len = k_ref.shape[1]
    load_keys(kx_ref, k_ref[0])
    store_queries(jnp.dot(ds_ref[0], kx_ref[...], preferred_element_type=F32), dq_refs)
    qt = q.T
    for h in range(HEADS):
        rows, at = slice(h * HEAD_DIM, (h + 1) * HEAD_DIM), slice(h * key_len, (h + 1) * key_len)
        dv_ref[rows] = dv_first[0, rows] + dv_in[0, rows]
        dk = jnp.dot(qt[rows], ds_ref[0, :, at], preferred_element_type=F32)
        dk_ref[rows] = (dk + dk_in[0, rows]) * SCALE
    dv_out[0] = dv_ref[...].T.astype(BF16)
    dk_out[0] = dk_ref[...].T.astype(BF16)


def grads(kind, col, parts, bias, chunk, keys, values, row_gate, stats, carried=()):
    rows, key_len, _ = keys.shape
    part_len = parts[0].shape[2]
    count, width = 4 * part_len, HEADS * key_len
    per_row = lambda i, *col: (i, 0, 0)
    whole = lambda i, *col: (0, 0)
    data = pl.BlockSpec((1, key_len, CH), per_row)
    side = pl.BlockSpec((1, CH, key_len), per_row)
    side_shape = jax.ShapeDtypeStruct((rows, CH, key_len), F32)
    data_shape = jax.ShapeDtypeStruct(keys.shape, BF16)
    square = pl.BlockSpec((1, count, width), per_row)
    square_shape = jax.ShapeDtypeStruct((rows, count, width), BF16)
    dq_specs = [pl.BlockSpec((2, 1, part_len, CH), lambda i, *col: (0, i, 0, 0))] * 2
    dq_shapes = [jax.ShapeDtypeStruct((2, rows, part_len, CH), BF16)] * 2
    db_spec = pl.BlockSpec((4, part_len, width), lambda i, *col: (0, 0, 0))
    db_shape = jax.ShapeDtypeStruct((4, part_len, width), BF16)
    stat_specs = [pl.BlockSpec((4, 1, 2 * HEADS, part_len), lambda i, col: (0, i, 0, 0))] * 4
    keys_scratch = pltpu.VMEM((width, 2 * CH), BF16)
    wide, low = pltpu.VMEM((count, width), F32), pltpu.VMEM((count, width), BF16)
    flops = rows * count * width * 512
    if kind == "products":
        return pl.pallas_call(
            products_kernel,
            grid=(rows,),
            in_specs=[pl.BlockSpec((2, 1, part_len, CH), lambda i: (0, i, 0, 0))] * 4
            + [data, side, square, side, side],
            out_specs=dq_specs + [data, data],
            out_shape=dq_shapes + [data_shape, data_shape],
            scratch_shapes=[pltpu.VMEM((width, CH), BF16), pltpu.VMEM((CH, key_len), F32), pltpu.VMEM((CH, key_len), F32)],
            compiler_params=pltpu.CompilerParams(vmem_limit_bytes=VMEM),
            cost_estimate=pl.CostEstimate(flops=flops * 3, bytes_accessed=2**20, transcendentals=0),
            name="products",
        )(*parts, keys, *carried)
    in_specs = part_specs(part_len, bias, chunk) + [data, data, pl.BlockSpec((8, key_len), whole)] + stat_specs
    if kind == "chances":
        out_specs, out_shape = [side, square, db_spec], [side_shape, square_shape, db_shape]
        scratch = [keys_scratch, keys_scratch, wide, wide, low]
    else:
        out_specs = dq_specs + [side, side, db_spec]
        out_shape = dq_shapes + [side_shape, side_shape, db_shape]
        scratch = [keys_scratch, keys_scratch, wide, low, low, wide]
    return pl.pallas_call(
        chances_kernel if kind == "chances" else grads_kernel,
        grid_spec=pltpu.PrefetchScalarGridSpec(
            num_scalar_prefetch=1, grid=(rows,), in_specs=in_specs, out_specs=out_specs, scratch_shapes=scratch
        ),
        out_shape=out_shape,
        compiler_params=pltpu.CompilerParams(vmem_limit_bytes=VMEM),
        cost_estimate=pl.CostEstimate(flops=flops * (4 if kind == "chances" else 6), bytes_accessed=2**20, transcendentals=0),
        name=kind,
    )(col, *parts, *[bias] * 4, keys, values, row_gate, *stats)


def partner(x, distance):
    return lax.ppermute(x, "cols", [(c, c ^ distance) for c in range(4)])


def per_device(queries, keys, values, out_grad, pair_bias, token_mask, span_index):
    rows, key_len, _ = keys.shape
    col = lax.axis_index("cols")
    owners = 8
    span = key_len // owners
    step = span // CHUNKS
    part_len = owners * step
    count = 4 * part_len
    width = HEADS * key_len

    row_keep = lax.dynamic_slice_in_dim(token_mask, span_index[0] * rows, rows)
    masked = out_grad * row_keep.astype(BF16)[:, None, None]
    pairs = jnp.stack([queries, masked]).reshape(2, rows, owners, CHUNKS, step, CH)

    key_keep = lax.dynamic_slice_in_dim(token_mask, col * key_len, key_len) > 0
    gate = jnp.where(key_keep, F32(0.0), F32(-1e30))
    key_gate = jnp.broadcast_to(gate[:, None], (key_len, CH))
    row_gate = jnp.broadcast_to(gate[None, :], (8, key_len))
    bias = jnp.concatenate([pair_bias[:, h] for h in range(HEADS)], axis=1)
    bias = bias.reshape(4 * owners, CHUNKS, step, width).swapaxes(0, 1).reshape(CHUNKS, 4, part_len, width)
    col_id = col.astype(jnp.int32).reshape(1)

    tie = lax.optimization_barrier
    owns = [pairs[:, :, :, b].reshape(2, rows, part_len, CH) for b in range(CHUNKS)]

    def spread(own, far):
        return [own, partner(own, 1), far, partner(far, 1)]

    def call_totals(b):
        return totals(col_id, parts[b], bias, b, keys, values, key_gate)

    def all_stats(stat):
        return [stat] + [partner(stat, distance) for distance in (1, 2, 3)]

    def call_grads(kind, b, stats, carried=()):
        return grads(kind, col_id, parts[b], bias, b, keys, values, row_gate, stats, carried)

    def near_queries(dq):
        pair = dq[0].astype(F32) + partner(dq[1], 1).astype(F32)
        return pair[0], pair[1].astype(BF16)

    def far_queries(pair):
        return (pair[0] + partner(pair[1], 2).astype(F32)).astype(BF16)

    def swap_bias(db):
        return lax.all_to_all(db.reshape(32, step, width), "rows", 0, 0, tiled=True)

    def summed(terms):
        return jnp.sum(terms.astype(F32), axis=0)

    far0, bias = tie((partner(owns[0], 2), bias))
    far0, owns[1] = tie((far0, owns[1]))
    far1 = partner(owns[1], 2)
    parts = [spread(owns[0], far0), None]
    t0 = call_totals(0)
    far1, t0 = tie((far1, t0))
    parts[1] = spread(owns[1], far1)
    t1 = call_totals(1)
    s0, t1 = tie((all_stats(t0), t1))
    p, ds, db0 = call_grads("chances", 0, s0)
    db0, s1 = tie((db0, all_stats(t1)))
    *dq1, dk, dv, db1 = call_grads("grads", 1, s1)
    db0, dq1, db1 = tie((swap_bias(db0), dq1, db1))
    db1 = swap_bias(db1)
    n1, p = tie((near_queries(dq1), p))
    *dq0, key_grad, value_grad = call_grads("products", 0, (), (p, ds, dk, dv))
    q1, dq0 = tie((far_queries(n1), dq0))
    n0 = near_queries(dq0)
    queries_out = [far_queries(n0), q1]
    bias_out = [summed(db0), summed(db1)]
    query_grad = jnp.stack(queries_out).reshape(CHUNKS, rows, owners, step, CH)
    query_grad = query_grad.transpose(1, 2, 0, 3, 4).reshape(rows, key_len, CH)
    bias_grad = jnp.concatenate(bias_out, axis=0).reshape(span, HEADS, key_len)
    return (query_grad, key_grad, value_grad, bias_grad)


def solution(mesh):
    return jax.shard_map(
        per_device,
        mesh=mesh,
        in_specs=(
            P("rows", "cols", None),
            P("rows", "cols", None),
            P("rows", "cols", None),
            P("rows", "cols", None),
            P(None, None, "cols"),
            P(),
            P("rows"),
        ),
        out_specs=(
            P("rows", "cols", None),
            P("rows", "cols", None),
            P("rows", "cols", None),
            P("rows", None, "cols"),
        ),
        check_vma=False,
    )
```
